32 devices in a mesh: groups: 2 (over y), gz: 4 (over z), xy: 2 (over x), col: 2 (over core).
Axes of the slice: x: 2, y: 2, z: 4, core: 2. Of those that a mesh axis runs over, the one named last changes fastest.
Arguments:
- features: bfloat16 [8, 16, 256, 256], P(('groups', 'gz'), None, ('xy', 'col')), parts along dimension 0, may hold values from -24 to 24
- class_map: int32 [8, 256, 256], P(('groups', 'gz'), ('xy', 'col')), parts along dimension 0, may hold values from 0 to 3
- stiffness: float32 [4], replicated, may hold values from 0.2 to 2
- valid: int32 [8, 4], P('groups'), parts along dimension 0, may hold values 0 or 1
Outputs:
- displacement: float32 [8, 2, 256, 256], P(('groups', 'gz'), None, ('xy', 'col')), parts along dimension 0
- forward_flow: float32 [8, 2, 256, 256], P(('groups', 'gz'), None, ('xy', 'col')), parts along dimension 0
The draws below stay inside these ranges and needn't reach their ends.
There are 2 independent parts, one for each index of `groups`. The reference program is written for one: setup_inputs(seed, part) draws one part's arguments, and reference() takes and returns one part's arrays. A program takes and returns all parts, laid end to end along the dimension named above; an argument that names none is the same for every part. Nothing has to cross between parts.
All inputs are finite; a program needn't handle non-finite values.
Results may differ from the reference program's by a relative error of at most 0.0017.
Values may be sent and summed in bfloat16 or wider, within the bound.
A program may use at most 64 MiB of HBM per device.

```python
import math
import jax
import jax.numpy as jnp
from jax import lax

CHANNELS = 16
RADIUS = 6
CLASSES = 4
STEPS = 3
TILE_ROWS = 64
TILE_COLS = 256
TILES = 4
SECTIONS = 4
SECT_ROWS = 256


def draw_features(key, part):
    shape = (SECTIONS, CHANNELS, SECT_ROWS, TILE_COLS)
    values = jnp.clip(jax.random.normal(key, shape, jnp.float32), -4.0, 4.0)
    return values.astype(jnp.bfloat16)


def with_ends(entries, stream_key, low, top_value):
    longest = entries.shape.index(max(entries.shape))
    spots = []
    for shift in (0, 1):
        where = [jax.random.randint(jax.random.fold_in(stream_key, axis), (), 0, length) for axis, length in enumerate(entries.shape)]
        where[longest] = (where[longest] + shift) % entries.shape[longest]
        spots.append(tuple(where))
    return entries.at[spots[0]].set(low).at[spots[1]].set(top_value)


def setup_inputs(seed: int = 0, part: int = 0) -> dict:
    splits = jax.random.split(jax.random.key(seed), 5)
    own_keys = jax.random.split(jax.random.fold_in(splits[4], part), 5)
    return {
        "features": draw_features(jax.random.fold_in(jax.random.fold_in(splits[4], part), 71), part),
        "class_map": with_ends(jax.random.randint(own_keys[1], (SECTIONS, SECT_ROWS, TILE_COLS), 0, CLASSES), jax.random.fold_in(own_keys[1], 1), 0, CLASSES - 1).astype(jnp.int32),
        "stiffness": jnp.clip(jnp.exp(jax.random.uniform(splits[2], (CLASSES,), jnp.float32, math.log(0.2), math.log(2.0))), 0.2, 2.0),
        "valid": with_ends((jax.random.randint(own_keys[3], (SECTIONS, TILES), 0, 4) < 3).astype(jnp.int32), jax.random.fold_in(own_keys[3], 1), 0, 1),
    }


score_scale = 0.25
step_size = 0.1
saturation = 2.0

def expected(stacked):
    highest = lax.optimization_barrier(jnp.max(stacked, axis=0))
    weights = jnp.exp(stacked - highest)
    denominator = lax.optimization_barrier(jnp.sum(weights, axis=0))
    window = 2 * RADIUS + 1
    places = jnp.arange(window * window, dtype=jnp.int32)
    row_shift = (places // window - RADIUS).astype(jnp.float32)
    col_shift = (places % window - RADIUS).astype(jnp.float32)
    flow_row = lax.optimization_barrier(jnp.sum(weights * row_shift[:, None, None], axis=0)) / denominator
    flow_col = lax.optimization_barrier(jnp.sum(weights * col_shift[:, None, None], axis=0)) / denominator
    return jnp.stack([flow_row, flow_col])

def band_scores(center_band, window_band, height, breadth):
    scores = []
    for shift_row in range(2 * RADIUS + 1):
        for shift_col in range(2 * RADIUS + 1):
            scores.append(lax.optimization_barrier(jnp.sum(center_band * window_band[:, shift_row:shift_row + height, shift_col:shift_col + breadth], axis=0)))
    return score_scale * jnp.stack(scores)

def elastic_term(disp_pad, stiff_pad):
    middle = disp_pad[..., 1:-1, 1:-1]
    stiff_mid = stiff_pad[..., 1:-1, 1:-1]
    result = jnp.zeros_like(middle)
    for row_part, col_part in ((slice(2, None), slice(1, -1)), (slice(0, -2), slice(1, -1)), (slice(1, -1), slice(2, None)), (slice(1, -1), slice(0, -2))):
        neighbour_stiff = stiff_pad[..., row_part, col_part]
        result = result + 0.5 * (stiff_mid + neighbour_stiff) * (middle - disp_pad[..., row_part, col_part])
    return result

def spring(vector):
    return vector / jnp.sqrt(1.0 + lax.optimization_barrier(jnp.sum(vector * vector, axis=-3, keepdims=True)) / (saturation * saturation))

def section_flow(pair_items):
    center, other = pair_items
    padded = jnp.pad(other, ((0, 0), (RADIUS, RADIUS), (RADIUS, RADIUS)))
    height, breadth = (center.shape[1], center.shape[2])
    return expected(band_scores(center.astype(jnp.float32), padded.astype(jnp.float32), height, breadth))

def reference(features, class_map, stiffness, valid):
    blank = jnp.zeros_like(features[:1])
    nexts = jnp.concatenate([features[1:], blank], axis=0)
    priors = jnp.concatenate([blank, features[:-1]], axis=0)
    forward = lax.map(section_flow, (features, nexts))
    backward = lax.map(section_flow, (features, priors))
    valid_f = valid.astype(jnp.float32)
    link_all = valid_f * jnp.concatenate([valid_f[1:], jnp.zeros((1, TILES), jnp.float32)], axis=0)
    link_under = jnp.concatenate([jnp.zeros((1, TILES), jnp.float32), link_all[:-1]], axis=0)
    link_here = jnp.repeat(link_all, TILE_ROWS, axis=1)[:, None, :, None]
    link_below = jnp.repeat(link_under, TILE_ROWS, axis=1)[:, None, :, None]
    excess = link_here * forward - link_below * backward
    before = jnp.concatenate([jnp.zeros_like(excess[:1]), jnp.cumsum(excess[:-1], axis=0)], axis=0)
    displace = 0.5 * (before - link_below * backward)
    levels = jnp.arange(CLASSES, dtype=jnp.int32)
    stiff_field = lax.optimization_barrier(jnp.sum(jnp.where(class_map[None] == levels[:, None, None, None], stiffness[:, None, None, None], 0.0), axis=0))
    stiff_pad = jnp.pad(stiff_field, ((0, 0), (1, 1), (1, 1)))[:, None]
    for step_number in range(STEPS):
        disp_pad = jnp.pad(displace, ((0, 0), (0, 0), (1, 1), (1, 1)))
        elastic = elastic_term(disp_pad, stiff_pad)
        upper_disp = jnp.concatenate([displace[1:], jnp.zeros_like(displace[:1])], axis=0)
        lower_disp = jnp.concatenate([jnp.zeros_like(displace[:1]), displace[:-1]], axis=0)
        pull_up = link_here * spring(upper_disp - displace - forward)
        pull_down = link_below * spring(lower_disp - displace - backward)
        from_below = jnp.concatenate([jnp.zeros_like(pull_up[:1]), pull_up[:-1]], axis=0)
        from_above = jnp.concatenate([pull_down[1:], jnp.zeros_like(pull_down[:1])], axis=0)
        gradient = elastic - pull_up - pull_down + from_below + from_above
        displace = displace - step_size * gradient
    return (displace, forward)
```

```python
import math

import jax
import jax.numpy as jnp
from jax import lax
from jax.experimental import pallas as pl
from jax.experimental.pallas import tpu as pltpu
from jax.sharding import PartitionSpec as P

RADIUS = 6
STEPS = 3


score_scale = 0.25
step_size = 0.1
saturation = 2.0


def padded_2(cells, sides, width):
    for axis, dim in sides:
        count = lax.axis_size(axis)
        ends = count - 1
        head = lax.slice_in_dim(cells, 0, width, axis=dim)
        tail = lax.slice_in_dim(cells, cells.shape[dim] - width, cells.shape[dim], axis=dim)
        cells = jnp.concatenate(
            [
                lax.ppermute(tail, axis, [(i, (i + 1) % count) for i in range(ends)]),
                cells,
                lax.ppermute(head, axis, [((i + 1) % count, i) for i in range(ends)]),
            ],
            axis=dim,
        )
    return cells


def passed_along(value, axis, steps):
    count = lax.axis_size(axis)
    initial, last = (max(0, -steps), min(count, count - steps))
    return lax.ppermute(value, axis, [(source, source + steps) for source in range(initial, last)])


def shortened(shard):
    return jax.tree.map(lambda a: a.astype(jnp.bfloat16) if a.dtype == jnp.float32 else a, shard)


LANES = 128
EDGE = 8
SPAN = 2 * RADIUS + 1


def shifted(halves, amount, lane):
    count = len(halves)
    source = lane - amount
    turned = [pltpu.roll(half, lax.rem(amount + LANES, LANES), 1) for half in halves]
    blank = jnp.zeros_like(turned[0])
    inside = (source >= 0) & (source < LANES)
    results = []
    for k in range(count):
        lower = turned[k - 1] if k > 0 else blank
        upper = turned[k + 1] if k + 1 < count else blank
        wrapped = jnp.where(source < 0, lower, upper)
        results.append(jnp.where(inside, turned[k], wrapped))
    return results


def flow_kernel(
    center_ref, other_ref, forward_ref, ahead_ref, center, other, turned, spill, score_f, score_b, top_f, top_b
):
    channels, padded_rows, breadth = center_ref.shape
    parts = breadth // LANES
    height = padded_rows - 2 * EDGE
    other_rows = other_ref.shape[1]
    lane = lax.broadcasted_iota(jnp.int32, (8, LANES), 1)
    factor = score_scale * math.log2(math.e)

    @pl.loop(0, channels)
    def _(c):
        for k in range(parts):
            cols = slice(k * LANES, (k + 1) * LANES)
            center[c, k] = center_ref[c, :, cols].astype(jnp.float32) * factor
            other[c, k] = other_ref[c, :, cols].astype(jnp.float32)

    top_f[...] = jnp.full(top_f.shape, -jnp.inf, jnp.float32)
    top_b[...] = jnp.full(top_b.shape, -jnp.inf, jnp.float32)

    @pl.loop(0, SPAN)
    def _(col):
        shift = col - RADIUS
        long_lane = lax.broadcasted_iota(jnp.int32, (other_rows, LANES), 1)

        @pl.loop(0, channels)
        def _(c):
            moved = shifted([other[c, k] for k in range(parts)], -shift, long_lane)
            for k in range(parts):
                turned[c, k] = moved[k]

        @pl.loop(0, padded_rows // 16)
        def _(pair):
            base = pl.multiple_of(pair * 16, 16)
            for k in range(parts):
                sums = [[None] * SPAN for _ in range(2)]
                for c in range(channels):
                    mine = [center[c, k, pl.ds(base + 8 * j, 8), :] for j in range(2)]
                    for offset in range(SPAN + 8):
                        window = turned[c, k, pl.ds(base + EDGE - RADIUS + offset, 8), :]
                        for j in range(2):
                            row = offset - 8 * j
                            if 0 <= row < SPAN:
                                term = mine[j] * window
                                sums[j][row] = term if c == 0 else sums[j][row] + term
                for j in range(2):
                    for row in range(SPAN):
                        spill[row, k, pl.ds(base + 8 * j, 8), :] = sums[j][row]

        @pl.loop(0, height // 8)
        def _(block):
            base = pl.multiple_of(block * 8, 8)
            here = pl.ds(base, 8)
            best_f = [top_f[k, here, :] for k in range(parts)]
            best_b = [top_b[k, here, :] for k in range(parts)]
            for row in range(SPAN):
                for k in range(parts):
                    value = spill[row, k, pl.ds(base + EDGE, 8), :]
                    score_f[col, row, k, here, :] = value
                    best_f[k] = jnp.maximum(best_f[k], value)
                back = shifted(
                    [spill[row, k, pl.ds(base + EDGE + RADIUS - row, 8), :] for k in range(parts)],
                    shift,
                    lane,
                )
                for k in range(parts):
                    score_b[col, row, k, here, :] = back[k]
                    best_b[k] = jnp.maximum(best_b[k], back[k])
            for k in range(parts):
                top_f[k, here, :] = best_f[k]
                top_b[k, here, :] = best_b[k]

    for score, top, out_ref, sign in (
        (score_f, top_f, forward_ref, 1.0),
        (score_b, top_b, ahead_ref, -1.0),
    ):

        @pl.loop(0, height // 8)
        def _(block):
            here = pl.ds(pl.multiple_of(block * 8, 8), 8)
            for k in range(parts):
                best = top[k, here, :]

                def one_column(col, carry):
                    total, along_rows, along_cols = carry
                    weights = [jnp.exp2(score[col, row, k, here, :] - best) for row in range(SPAN)]
                    summed = weights[RADIUS]
                    lean = None
                    for step in range(1, RADIUS + 1):
                        up, down = weights[RADIUS + step], weights[RADIUS - step]
                        summed = summed + (up + down)
                        part = (up - down) * float(step)
                        lean = part if lean is None else lean + part
                    place = (col - RADIUS).astype(jnp.float32)
                    return total + summed, along_rows + lean, along_cols + summed * place

                zero = jnp.zeros((8, LANES), jnp.float32)
                total, along_rows, along_cols = lax.fori_loop(
                    0, SPAN, one_column, (zero, zero, zero)
                )
                cols = slice(k * LANES, (k + 1) * LANES)
                out_ref[0, here, cols] = sign * along_rows / total
                out_ref[1, here, cols] = sign * along_cols / total


def flows_between(center, other):
    channels, padded_rows, breadth = center.shape
    other_rows = other.shape[1]
    parts = breadth // LANES
    height = padded_rows - 2 * EDGE
    shape = jax.ShapeDtypeStruct((2, height, breadth), jnp.float32)
    vmem = pl.BlockSpec(memory_space=pltpu.VMEM)
    return pl.pallas_call(
        flow_kernel,
        out_shape=(shape, shape),
        in_specs=[vmem, vmem],
        out_specs=(vmem, vmem),
        scratch_shapes=[
            pltpu.VMEM((channels, parts, padded_rows, LANES), jnp.float32),
            pltpu.VMEM((channels, parts, other_rows, LANES), jnp.float32),
            pltpu.VMEM((channels, parts, other_rows, LANES), jnp.float32),
            pltpu.VMEM((SPAN, parts, padded_rows, LANES), jnp.float32),
            pltpu.VMEM((SPAN, SPAN, parts, height, LANES), jnp.float32),
            pltpu.VMEM((SPAN, SPAN, parts, height, LANES), jnp.float32),
            pltpu.VMEM((parts, height, LANES), jnp.float32),
            pltpu.VMEM((parts, height, LANES), jnp.float32),
        ],
        compiler_params=pltpu.CompilerParams(vmem_limit_bytes=48 * 1024 * 1024),
    )(center, other)


def sent(value, up, along):
    axes = ("gz", "xy", "col")
    sections = lax.axis_size("gz")
    tiles = lax.axis_size(("xy", "col"))
    pairs = [
        (z * tiles + t, (z + up) * tiles + t + along)
        for z in range(sections)
        for t in range(tiles)
        if 0 <= z + up < sections and 0 <= t + along < tiles
    ]
    return lax.ppermute(value, axes, pairs)


def margins(middle, before, after, edge):
    channels, rows, breadth = middle.shape
    blank = jnp.zeros((channels, edge - RADIUS, breadth), middle.dtype)
    return jnp.concatenate([blank, before, middle, after, blank], axis=1)


def widen(values_in, margin):
    padding = [(0, 0)] * (values_in.ndim - 1) + [(margin, margin)]
    return jnp.pad(values_in, padding)


def elastic_term(disp_pad, stiff_pad):
    middle = disp_pad[..., 1:-1, 1:-1]
    stiff_mid = stiff_pad[..., 1:-1, 1:-1]
    result = jnp.zeros_like(middle)
    for row_part, col_part in (
        (slice(2, None), slice(1, -1)),
        (slice(0, -2), slice(1, -1)),
        (slice(1, -1), slice(2, None)),
        (slice(1, -1), slice(0, -2)),
    ):
        neighbour_stiff = stiff_pad[..., row_part, col_part]
        result = result + 0.5 * (stiff_mid + neighbour_stiff) * (
            middle - disp_pad[..., row_part, col_part]
        )
    return result


def spring(vector):
    return vector / jnp.sqrt(
        1.0 + jnp.sum(vector * vector, axis=-3, keepdims=True) / (saturation * saturation)
    )


def on_device(features, class_map, stiffness, valid):
    center = features[0]
    height, breadth = (center.shape[1], center.shape[2])
    section = lax.axis_index("gz")
    tile_index = lax.axis_index(("xy", "col"))
    column = lax.dynamic_slice_in_dim(valid, tile_index, 1, 1)[:, 0].astype(jnp.float32)
    link_all = column * jnp.concatenate([column[1:], jnp.zeros((1,), jnp.float32)])
    link_here = lax.dynamic_index_in_dim(link_all, section, 0, keepdims=False)
    link_below = jnp.where(
        section > 0,
        lax.dynamic_index_in_dim(link_all, jnp.maximum(section - 1, 0), 0, keepdims=False),
        0.0,
    )
    head, tail = (center[:, :RADIUS], center[:, height - RADIUS :])
    other = margins(sent(center, -1, 0), sent(tail, -1, 1), sent(head, -1, -1), 2 * EDGE)
    padded = margins(center, sent(tail, 0, 1), sent(head, 0, -1), EDGE)
    forward, ahead_flow = flows_between(padded, other)
    passed = passed_along(jnp.stack([forward, ahead_flow]), "gz", 1)
    prior_flow = passed[0]
    backward = passed[1]
    gathered = lax.all_gather(link_here * (forward - ahead_flow), "gz")
    earlier = (jnp.arange(gathered.shape[0]) < section)[:, None, None, None]
    displace = 0.5 * jnp.sum(jnp.where(earlier, gathered, 0.0), axis=0)
    levels = jnp.arange(stiffness.shape[0], dtype=jnp.int32)
    stiff_field = jnp.sum(
        jnp.where(class_map[0][None] == levels[:, None, None], stiffness[:, None, None], 0.0),
        axis=0,
    )
    stiff_pad = widen(padded_2(stiff_field, ((("xy", "col"), 0),), 1), 1)
    for step_number in range(STEPS):
        disp_pad = widen(padded_2(displace, ((("xy", "col"), 1),), 1), 1)
        elastic = elastic_term(disp_pad, stiff_pad)
        upper_disp = passed_along(shortened(displace), "gz", -1).astype(displace.dtype)
        lower_disp = passed_along(shortened(displace), "gz", 1).astype(displace.dtype)
        pull_up = link_here * spring(upper_disp - displace - forward)
        pull_down = link_below * spring(lower_disp - displace - backward)
        from_below = link_below * spring(displace - lower_disp - prior_flow)
        from_above = link_here * spring(displace - upper_disp - ahead_flow)
        gradient = elastic - pull_up - pull_down + from_below + from_above
        displace = displace - step_size * gradient
    return (displace[None], forward[None])


def solution(mesh):
    placed = (
        P(("groups", "gz"), None, ("xy", "col"), None),
        P(("groups", "gz"), ("xy", "col"), None),
        P(),
        P("groups", None),
    )
    return jax.shard_map(
        on_device,
        mesh=mesh,
        in_specs=placed,
        out_specs=(
            P(("groups", "gz"), None, ("xy", "col"), None),
            P(("groups", "gz"), None, ("xy", "col"), None),
        ),
        check_vma=False,
    )
```

```python
import math

import jax
import jax.numpy as jnp
from jax import lax
from jax.experimental import pallas as pl
from jax.experimental.pallas import tpu as pltpu
from jax.sharding import PartitionSpec as P

RADIUS = 6
STEPS = 3


score_scale = 0.25
step_size = 0.1
saturation = 2.0


LANES = 128
EDGE = 8
SPAN = 2 * RADIUS + 1


def shifted(halves, amount, lane):
    count = len(halves)
    source = lane - amount
    turned = [pltpu.roll(half, lax.rem(amount + LANES, LANES), 1) for half in halves]
    blank = jnp.zeros_like(turned[0])
    inside = (source >= 0) & (source < LANES)
    results = []
    for k in range(count):
        lower = turned[k - 1] if k > 0 else blank
        upper = turned[k + 1] if k + 1 < count else blank
        wrapped = jnp.where(source < 0, lower, upper)
        results.append(jnp.where(inside, turned[k], wrapped))
    return results


def flow_kernel(
    center_ref, other_ref, forward_ref, ahead_ref, center, other, turned, spill, score_f, score_b, top_f, top_b
):
    channels, padded_rows, breadth = center_ref.shape
    parts = breadth // LANES
    height = padded_rows - 2 * EDGE
    other_rows = other_ref.shape[1]
    lane = lax.broadcasted_iota(jnp.int32, (8, LANES), 1)
    factor = score_scale * math.log2(math.e)

    @pl.loop(0, channels)
    def _(c):
        for k in range(parts):
            cols = slice(k * LANES, (k + 1) * LANES)
            center[c, k] = center_ref[c, :, cols].astype(jnp.float32) * factor
            other[c, k] = other_ref[c, :, cols].astype(jnp.float32)

    top_f[...] = jnp.full(top_f.shape, -jnp.inf, jnp.float32)
    top_b[...] = jnp.full(top_b.shape, -jnp.inf, jnp.float32)

    @pl.loop(0, SPAN)
    def _(col):
        shift = col - RADIUS
        long_lane = lax.broadcasted_iota(jnp.int32, (other_rows, LANES), 1)

        @pl.loop(0, channels)
        def _(c):
            moved = shifted([other[c, k] for k in range(parts)], -shift, long_lane)
            for k in range(parts):
                turned[c, k] = moved[k]

        @pl.loop(0, padded_rows // 16)
        def _(pair):
            base = pl.multiple_of(pair * 16, 16)
            for k in range(parts):
                sums = [[None] * SPAN for _ in range(2)]
                for c in range(channels):
                    mine = [center[c, k, pl.ds(base + 8 * j, 8), :] for j in range(2)]
                    for offset in range(SPAN + 8):
                        window = turned[c, k, pl.ds(base + EDGE - RADIUS + offset, 8), :]
                        for j in range(2):
                            row = offset - 8 * j
                            if 0 <= row < SPAN:
                                term = mine[j] * window
                                sums[j][row] = term if c == 0 else sums[j][row] + term
                for j in range(2):
                    for row in range(SPAN):
                        spill[row, k, pl.ds(base + 8 * j, 8), :] = sums[j][row]

        @pl.loop(0, height // 8)
        def _(block):
            base = pl.multiple_of(block * 8, 8)
            here = pl.ds(base, 8)
            best_f = [top_f[k, here, :] for k in range(parts)]
            best_b = [top_b[k, here, :] for k in range(parts)]
            for row in range(SPAN):
                for k in range(parts):
                    value = spill[row, k, pl.ds(base + EDGE, 8), :]
                    score_f[col, row, k, here, :] = value
                    best_f[k] = jnp.maximum(best_f[k], value)
                back = shifted(
                    [spill[row, k, pl.ds(base + EDGE + RADIUS - row, 8), :] for k in range(parts)],
                    shift,
                    lane,
                )
                for k in range(parts):
                    score_b[col, row, k, here, :] = back[k]
                    best_b[k] = jnp.maximum(best_b[k], back[k])
            for k in range(parts):
                top_f[k, here, :] = best_f[k]
                top_b[k, here, :] = best_b[k]

    for score, top, out_ref, sign in (
        (score_f, top_f, forward_ref, 1.0),
        (score_b, top_b, ahead_ref, -1.0),
    ):

        @pl.loop(0, height // 8)
        def _(block):
            here = pl.ds(pl.multiple_of(block * 8, 8), 8)
            for k in range(parts):
                best = top[k, here, :]

                def one_column(col, carry):
                    total, along_rows, along_cols = carry
                    weights = [jnp.exp2(score[col, row, k, here, :] - best) for row in range(SPAN)]
                    summed = weights[RADIUS]
                    lean = None
                    for step in range(1, RADIUS + 1):
                        up, down = weights[RADIUS + step], weights[RADIUS - step]
                        summed = summed + (up + down)
                        part = (up - down) * float(step)
                        lean = part if lean is None else lean + part
                    place = (col - RADIUS).astype(jnp.float32)
                    return total + summed, along_rows + lean, along_cols + summed * place

                zero = jnp.zeros((8, LANES), jnp.float32)
                total, along_rows, along_cols = lax.fori_loop(
                    0, SPAN, one_column, (zero, zero, zero)
                )
                cols = slice(k * LANES, (k + 1) * LANES)
                out_ref[0, here, cols] = sign * along_rows / total
                out_ref[1, here, cols] = sign * along_cols / total


def flows_between(center, other):
    channels, padded_rows, breadth = center.shape
    other_rows = other.shape[1]
    parts = breadth // LANES
    height = padded_rows - 2 * EDGE
    shape = jax.ShapeDtypeStruct((2, height, breadth), jnp.float32)
    vmem = pl.BlockSpec(memory_space=pltpu.VMEM)
    return pl.pallas_call(
        flow_kernel,
        out_shape=(shape, shape),
        in_specs=[vmem, vmem],
        out_specs=(vmem, vmem),
        scratch_shapes=[
            pltpu.VMEM((channels, parts, padded_rows, LANES), jnp.float32),
            pltpu.VMEM((channels, parts, other_rows, LANES), jnp.float32),
            pltpu.VMEM((channels, parts, other_rows, LANES), jnp.float32),
            pltpu.VMEM((SPAN, parts, padded_rows, LANES), jnp.float32),
            pltpu.VMEM((SPAN, SPAN, parts, height, LANES), jnp.float32),
            pltpu.VMEM((SPAN, SPAN, parts, height, LANES), jnp.float32),
            pltpu.VMEM((parts, height, LANES), jnp.float32),
            pltpu.VMEM((parts, height, LANES), jnp.float32),
        ],
        compiler_params=pltpu.CompilerParams(vmem_limit_bytes=48 * 1024 * 1024),
    )(center, other)


def sent(value, up, along):
    axes = ("gz", "xy", "col")
    sections = lax.axis_size("gz")
    tiles = lax.axis_size(("xy", "col"))
    pairs = [
        (z * tiles + t, (z + up) * tiles + t + along)
        for z in range(sections)
        for t in range(tiles)
        if 0 <= z + up < sections and 0 <= t + along < tiles
    ]
    return lax.ppermute(value, axes, pairs)


def margins(middle, before, after, edge):
    channels, rows, breadth = middle.shape
    blank = jnp.zeros((channels, edge - RADIUS, breadth), middle.dtype)
    return jnp.concatenate([blank, before, middle, after, blank], axis=1)


def spread(first, second):
    return lax.rsqrt(1.0 + (first * first + second * second) / (saturation * saturation))


def relax_kernel(
    links_ref,
    forward_ref,
    ahead_ref,
    stiff_ref,
    out_ref,
    stiff,
    disp,
    prior,
    backward,
    summed,
    summed_in,
    above,
    below,
    rounded,
    above_in,
    below_in,
    flow_send,
    flow_recv,
    sum_send,
    sum_recv,
    stiff_send,
    stiff_recv,
    row_send,
    row_recv,
    sect_send,
    sect_recv,
):
    height, breadth = stiff_ref.shape
    sections = lax.axis_size("gz")
    wide = lax.axis_size("col")
    tiles = lax.axis_size("xy") * wide
    section = lax.axis_index("gz")
    tile = lax.axis_index("xy") * wide + lax.axis_index("col")
    link_here = links_ref[0]
    link_below = links_ref[1]

    def tile_at(t):
        return {"xy": t // wide, "col": lax.rem(t, wide)}

    next_tile, prior_tile = tile_at(tile + 1), tile_at(tile + tiles - 1 - tiles * (tile > 0))
    next_section, prior_section = {"gz": section + 1}, {"gz": section - 1}
    has_next_tile, has_prior_tile = tile + 1 < tiles, tile > 0
    has_next, has_prior = section + 1 < sections, section > 0
    partners = (
        (has_next_tile, next_tile),
        (has_prior_tile, prior_tile),
        (has_next, next_section),
        (has_prior, prior_section),
    )

    top, bottom = slice(0, EDGE), slice(EDGE + height, 2 * EDGE + height)
    first, last = slice(EDGE, 2 * EDGE), slice(height, EDGE + height)
    for edge in (top, bottom):
        stiff[edge, :] = jnp.zeros((EDGE, breadth), jnp.float32)
        for step in range(STEPS):
            for part in range(2):
                disp[step, part, edge, :] = jnp.zeros((EDGE, breadth), jnp.float32)
    for array in (prior, backward, summed_in):
        array[...] = jnp.zeros(array.shape, array.dtype)
    above_in[...] = jnp.zeros(above_in.shape, above_in.dtype)
    below_in[...] = jnp.zeros(below_in.shape, below_in.dtype)
    stiff[EDGE : EDGE + height, :] = stiff_ref[...]

    barrier = pltpu.get_barrier_semaphore()
    count = jnp.int32(0)
    for present, partner in partners:
        count = count + present.astype(jnp.int32)

        @pl.when(present)
        def _():
            pl.semaphore_signal(
                barrier, inc=1, device_id=partner, device_id_type=pl.DeviceIdType.MESH
            )

    pl.semaphore_wait(barrier, count)

    pending = []

    def send(condition, source, target, send_sem, recv_sem, partner):
        copy = pltpu.make_async_remote_copy(
            src_ref=source,
            dst_ref=target,
            send_sem=send_sem,
            recv_sem=recv_sem,
            device_id=partner,
            device_id_type=pl.DeviceIdType.MESH,
        )

        @pl.when(condition)
        def _():
            copy.start()

        pending.append((condition, copy))
        return copy

    def arrive(condition, copy):
        @pl.when(condition)
        def _():
            copy.wait_recv()

    flows = []
    for part in range(2):
        pieces = []
        for which, (source, target) in enumerate(((forward_ref, prior), (ahead_ref, backward))):
            pieces.append(
                send(
                    has_next,
                    source.at[part],
                    target.at[part],
                    flow_send.at[part, which],
                    flow_recv.at[part, which],
                    next_section,
                )
            )
        flows.append(pieces)
    stiff_down = send(
        has_next_tile, stiff.at[last], stiff.at[top], stiff_send.at[0], stiff_recv.at[0], next_tile
    )
    stiff_up = send(
        has_prior_tile, stiff.at[first], stiff.at[bottom], stiff_send.at[1], stiff_recv.at[1], prior_tile
    )

    def send_rows(step):
        down = send(
            has_next_tile,
            disp.at[step, :, last],
            disp.at[step, :, top],
            row_send.at[step, 0],
            row_recv.at[step, 0],
            next_tile,
        )
        up = send(
            has_prior_tile,
            disp.at[step, :, first],
            disp.at[step, :, bottom],
            row_send.at[step, 1],
            row_recv.at[step, 1],
            prior_tile,
        )
        return down, up

    for part in range(2):
        for copy in flows[part]:
            arrive(has_prior, copy)
        chain = pltpu.make_async_remote_copy(
            src_ref=summed.at[part],
            dst_ref=summed_in.at[part],
            send_sem=sum_send.at[part],
            recv_sem=sum_recv.at[part],
            device_id=next_section,
            device_id_type=pl.DeviceIdType.MESH,
        )
        arrive(section > 1, chain)
        before = summed_in[part]
        here = before + link_below * (prior[part] - backward[part])
        summed[part] = here
        send(
            has_next & has_prior,
            summed.at[part],
            summed_in.at[part],
            sum_send.at[part],
            sum_recv.at[part],
            next_section,
        )
        disp[0, part, EDGE : EDGE + height, :] = 0.5 * here
        below[part] = 0.5 * before
        above[part] = 0.5 * (here + link_here * (forward_ref[part] - ahead_ref[part]))

    rows = send_rows(0)
    arrive(has_prior_tile, stiff_down)
    arrive(has_next_tile, stiff_up)
    lane = lax.broadcasted_iota(jnp.int32, (16, breadth), 1)
    at_left, at_right = lane == 0, lane == breadth - 1

    def left_of(value):
        return jnp.where(at_left, 0.0, pltpu.roll(value, 1, 1))

    def right_of(value):
        return jnp.where(at_right, 0.0, pltpu.roll(value, breadth - 1, 1))

    crossing = None
    for step in range(STEPS):
        arrive(has_prior_tile, rows[0])
        arrive(has_next_tile, rows[1])
        if crossing is not None:
            arrive(has_next, crossing[0])
            arrive(has_prior, crossing[1])

        @pl.loop(0, height // 16)
        def _(block):
            base = pl.multiple_of(block * 16, 16)
            here = pl.ds(base, 16)
            inner = pl.ds(pl.multiple_of(base + EDGE, EDGE), 16)
            around = pl.ds(base, 16 + 2 * EDGE)
            stiff_all = stiff[around, :]
            middle_stiff = stiff_all[EDGE : EDGE + 16]
            weights = [
                0.5 * (middle_stiff + neighbour)
                for neighbour in (
                    stiff_all[EDGE + 1 : EDGE + 17],
                    stiff_all[EDGE - 1 : EDGE + 15],
                    right_of(middle_stiff),
                    left_of(middle_stiff),
                )
            ]
            windows = [disp[step, part, around, :] for part in range(2)]
            middles = [window[EDGE : EDGE + 16] for window in windows]
            if step == 0:
                uppers = [above[part, here, :] for part in range(2)]
                lowers = [below[part, here, :] for part in range(2)]
            else:
                uppers = [above_in[step - 1, part, here, :].astype(jnp.float32) for part in range(2)]
                lowers = [below_in[step - 1, part, here, :].astype(jnp.float32) for part in range(2)]
            gradients = []
            for part in range(2):
                middle = middles[part]
                neighbours = (
                    windows[part][EDGE + 1 : EDGE + 17],
                    windows[part][EDGE - 1 : EDGE + 15],
                    right_of(middle),
                    left_of(middle),
                )
                total = weights[0] * (middle - neighbours[0])
                for k in range(1, 4):
                    total = total + weights[k] * (middle - neighbours[k])
                gradients.append(total)
            for sign, link, others, flow in (
                (-1.0, link_here, uppers, forward_ref),
                (-1.0, link_below, lowers, backward),
                (1.0, link_below, lowers, prior),
                (1.0, link_here, uppers, ahead_ref),
            ):
                vector = [
                    -sign * (others[part] - middles[part]) - flow[part, here, :] for part in range(2)
                ]
                scale = (sign * link) * spread(*vector)
                for part in range(2):
                    gradients[part] = gradients[part] + scale * vector[part]
            for part in range(2):
                updated = middles[part] - step_size * gradients[part]
                if step == STEPS - 1:
                    out_ref[part, here, :] = updated
                else:
                    disp[step + 1, part, inner, :] = updated
                    rounded[step, part, here, :] = updated.astype(rounded.dtype)

        if step < STEPS - 1:
            crossing = (
                send(
                    has_prior,
                    rounded.at[step],
                    above_in.at[step],
                    sect_send.at[step, 0],
                    sect_recv.at[step, 0],
                    prior_section,
                ),
                send(
                    has_next,
                    rounded.at[step],
                    below_in.at[step],
                    sect_send.at[step, 1],
                    sect_recv.at[step, 1],
                    next_section,
                ),
            )
            rows = send_rows(step + 1)

    for condition, copy in pending:

        @pl.when(condition)
        def _():
            copy.wait_send()


def relaxed(links, forward, ahead, stiff_field):
    height, breadth = stiff_field.shape
    vmem = pl.BlockSpec(memory_space=pltpu.VMEM)
    pair = (2, height, breadth)
    moved = (STEPS - 1, 2, height, breadth)
    dma = pltpu.SemaphoreType.DMA
    return pl.pallas_call(
        relax_kernel,
        out_shape=jax.ShapeDtypeStruct(pair, jnp.float32),
        in_specs=[pl.BlockSpec(memory_space=pltpu.SMEM), vmem, vmem, vmem],
        out_specs=vmem,
        scratch_shapes=[
            pltpu.VMEM((height + 2 * EDGE, breadth), jnp.float32),
            pltpu.VMEM((STEPS, 2, height + 2 * EDGE, breadth), jnp.float32),
            *[pltpu.VMEM(pair, jnp.float32) for _ in range(6)],
            *[pltpu.VMEM(moved, jnp.bfloat16) for _ in range(3)],
            dma((2, 2)),
            dma((2, 2)),
            dma((2,)),
            dma((2,)),
            dma((2,)),
            dma((2,)),
            dma((STEPS, 2)),
            dma((STEPS, 2)),
            dma((STEPS - 1, 2)),
            dma((STEPS - 1, 2)),
        ],
        compiler_params=pltpu.CompilerParams(
            collective_id=0, has_side_effects=True, vmem_limit_bytes=16 * 1024 * 1024
        ),
    )(links, forward, ahead, stiff_field)


def on_device(features, class_map, stiffness, valid):
    center = features[0]
    height, breadth = (center.shape[1], center.shape[2])
    section = lax.axis_index("gz")
    tile_index = lax.axis_index(("xy", "col"))
    column = lax.dynamic_slice_in_dim(valid, tile_index, 1, 1)[:, 0].astype(jnp.float32)
    link_all = column * jnp.concatenate([column[1:], jnp.zeros((1,), jnp.float32)])
    link_here = lax.dynamic_index_in_dim(link_all, section, 0, keepdims=False)
    link_below = jnp.where(
        section > 0,
        lax.dynamic_index_in_dim(link_all, jnp.maximum(section - 1, 0), 0, keepdims=False),
        0.0,
    )
    head, tail = (center[:, :RADIUS], center[:, height - RADIUS :])
    other = margins(sent(center, -1, 0), sent(tail, -1, 1), sent(head, -1, -1), 2 * EDGE)
    padded = margins(center, sent(tail, 0, 1), sent(head, 0, -1), EDGE)
    forward, ahead_flow = flows_between(padded, other)
    levels = jnp.arange(stiffness.shape[0], dtype=jnp.int32)
    stiff_field = jnp.sum(
        jnp.where(class_map[0][None] == levels[:, None, None], stiffness[:, None, None], 0.0),
        axis=0,
    )
    displace = relaxed(jnp.stack([link_here, link_below]), forward, ahead_flow, stiff_field)
    return (displace[None], forward[None])


def solution(mesh):
    placed = (
        P(("groups", "gz"), None, ("xy", "col"), None),
        P(("groups", "gz"), ("xy", "col"), None),
        P(),
        P("groups", None),
    )
    return jax.shard_map(
        on_device,
        mesh=mesh,
        in_specs=placed,
        out_specs=(
            P(("groups", "gz"), None, ("xy", "col"), None),
            P(("groups", "gz"), None, ("xy", "col"), None),
        ),
        check_vma=False,
    )
```

```python
import math

import jax
import jax.numpy as jnp
from jax import lax
from jax.experimental import pallas as pl
from jax.experimental.pallas import tpu as pltpu
from jax.sharding import PartitionSpec as P

RADIUS = 6
STEPS = 3


score_scale = 0.25
step_size = 0.1
saturation = 2.0


LANES = 128
EDGE = 8
SPAN = 2 * RADIUS + 1
GROUP = 4
MANY = 8


def shifted(halves, turn, from_lower, from_upper):
    count = len(halves)
    turned = [pltpu.roll(half, turn, 1) for half in halves]
    blank = jnp.zeros_like(turned[0])
    results = []
    for k in range(count):
        lower = turned[k - 1] if k > 0 else blank
        upper = turned[k + 1] if k + 1 < count else blank
        results.append(jnp.where(from_lower, lower, jnp.where(from_upper, upper, turned[k])))
    return results


def flow_kernel(
    center_ref, other_ref, forward_ref, ahead_ref, center, turned, score_f, top_f, top_b
):
    channels, padded_rows, breadth = center_ref.shape
    parts = breadth // LANES
    height = padded_rows - 2 * EDGE
    other_rows = other_ref.shape[1]
    lane = lax.broadcasted_iota(jnp.int32, (8, LANES), 1)
    many = math.gcd(height // 8, MANY)
    together = math.gcd(channels, 16)
    factor = score_scale * math.log2(math.e)

    @pl.loop(0, channels)
    def _(c):
        for k in range(parts):
            cols = slice(k * LANES, (k + 1) * LANES)
            center[c, k, 0:padded_rows, :] = center_ref[c, :, cols].astype(jnp.float32) * factor

    top_f[...] = jnp.full(top_f.shape, -jnp.inf, jnp.float32)
    top_b[...] = jnp.full(top_b.shape, -jnp.inf, jnp.float32)

    @pl.loop(0, SPAN)
    def _(col):
        shift = col - RADIUS
        back_turn = lax.rem(LANES + shift, LANES)
        back_masks = (lane - shift < 0, lane - shift >= LANES)
        source = lax.broadcasted_iota(jnp.int32, (breadth, breadth), 0)
        target = lax.broadcasted_iota(jnp.int32, (breadth, breadth), 1)
        mover = jnp.where(source - target == shift, 1.0, 0.0).astype(jnp.bfloat16)

        @pl.loop(0, channels // together)
        def _(group):
            these = pl.ds(group * together, together)
            moved = jnp.dot(
                other_ref[these].reshape(together * other_rows, breadth),
                mover,
                preferred_element_type=jnp.float32,
            ).reshape(together, other_rows, breadth)
            for k in range(parts):
                turned[these, k] = moved[:, :, k * LANES : (k + 1) * LANES]

        @pl.loop(0, padded_rows // 16)
        def _(pair):
            base = pl.multiple_of(pair * 16, 16)
            for k in range(parts):
                sums = [[None] * SPAN for _ in range(2)]
                for c in range(channels):
                    mine = {}
                    windows = {}
                    for j in range(2):
                        for row in range(SPAN):
                            near = (RADIUS - (row - RADIUS)) % GROUP
                            far = 8 * j + EDGE + row - RADIUS + near
                            if (j, near) not in mine:
                                mine[j, near] = center[c, k, pl.ds(base + 8 * j + near, 8), :]
                            if far not in windows:
                                windows[far] = turned[c, k, pl.ds(base + far, 8), :]
                            term = mine[j, near] * windows[far]
                            sums[j][row] = term if c == 0 else sums[j][row] + term
                for j in range(2):
                    for row in range(SPAN):
                        near = (RADIUS - (row - RADIUS)) % GROUP
                        score_f[col, row, k, pl.ds(base + 8 * j + near, 8), :] = sums[j][row]

        @pl.loop(0, height // (8 * many))
        def _(chunk):
            raw = []
            for j in range(many):
                base = pl.multiple_of(chunk * (8 * many) + 8 * j, 8)
                here = pl.ds(base, 8)
                bests_f, bests_b = [None] * parts, [None] * parts
                for k in range(parts):
                    for row in range(SPAN):
                        value = score_f[col, row, k, pl.ds(base + EDGE, 8), :]
                        other = score_f[col, row, k, pl.ds(base + EDGE + RADIUS - row, 8), :]
                        bests_f[k] = value if row == 0 else jnp.maximum(bests_f[k], value)
                        bests_b[k] = other if row == 0 else jnp.maximum(bests_b[k], other)
                    top_f[k, here, :] = jnp.maximum(top_f[k, here, :], bests_f[k])
                raw.append((here, bests_b))
            turned_back = [(here, shifted(values, back_turn, *back_masks)) for here, values in raw]
            for here, values in turned_back:
                for k in range(parts):
                    top_b[k, here, :] = jnp.maximum(top_b[k, here, :], values[k])

    @pl.loop(0, height // (8 * many))
    def _(chunk):
        bases = [pl.multiple_of(chunk * (8 * many) + 8 * j, 8) for j in range(many)]
        bests_f = [[top_f[k, pl.ds(base, 8), :] for k in range(parts)] for base in bases]
        bests_b = [[top_b[k, pl.ds(base, 8), :] for k in range(parts)] for base in bases]

        def sums_of(scores, best, sign):
            weights = [jnp.exp2(score - best) for score in scores]
            summed = weights[RADIUS]
            lean = None
            for step in range(1, RADIUS + 1):
                up, down = weights[RADIUS + step], weights[RADIUS - step]
                summed = summed + (up + down)
                part = (up - down) * (sign * step)
                lean = part if lean is None else lean + part
            return summed, lean

        def one_column(col, carry):
            shift = col - RADIUS
            place = shift.astype(jnp.float32)
            forth_turn = lax.rem(LANES - shift, LANES)
            back_turn = lax.rem(LANES + shift, LANES)
            forth_masks = (lane + shift < 0, lane + shift >= LANES)
            back_masks = (lane - shift < 0, lane - shift >= LANES)
            moved = [shifted(best, forth_turn, *forth_masks) for best in bests_b]
            forward = [
                [
                    sums_of(
                        [score_f[col, row, k, pl.ds(base + EDGE, 8), :] for row in range(SPAN)],
                        bests_f[j][k],
                        1.0,
                    )
                    for k in range(parts)
                ]
                for j, base in enumerate(bases)
            ]
            back = [
                [
                    sums_of(
                        [
                            score_f[col, row, k, pl.ds(base + EDGE + RADIUS - row, 8), :]
                            for row in range(SPAN)
                        ],
                        moved[j][k],
                        -1.0,
                    )
                    for k in range(parts)
                ]
                for j, base in enumerate(bases)
            ]
            turned_back = [
                [shifted([value[i] for value in row], back_turn, *back_masks) for i in range(2)]
                for row in back
            ]
            results = []
            for j in range(many):
                for k in range(parts):
                    column = lane + (k * LANES - shift)
                    inside = (column >= 0) & (column < breadth)
                    outside = float(SPAN) * jnp.exp2(-bests_b[j][k])
                    summed = jnp.where(inside, turned_back[j][0][k], outside)
                    lean = jnp.where(inside, turned_back[j][1][k], 0.0)
                    old = carry[j * parts + k]
                    ahead_sum, ahead_lean = forward[j][k]
                    results.append(
                        (
                            old[0] + ahead_sum,
                            old[1] + ahead_lean,
                            old[2] + ahead_sum * place,
                            old[3] + summed,
                            old[4] + lean,
                            old[5] - summed * place,
                        )
                    )
            return tuple(results)

        zero = jnp.zeros((8, LANES), jnp.float32)
        results = lax.fori_loop(0, SPAN, one_column, ((zero,) * 6,) * (many * parts))
        for j, base in enumerate(bases):
            for k in range(parts):
                cols = slice(k * LANES, (k + 1) * LANES)
                sums = results[j * parts + k]
                for out_ref, (total, along_rows, along_cols) in (
                    (forward_ref, sums[:3]),
                    (ahead_ref, sums[3:]),
                ):
                    out_ref[0, pl.ds(base, 8), cols] = along_rows / total
                    out_ref[1, pl.ds(base, 8), cols] = along_cols / total


def flows_between(center, other):
    channels, padded_rows, breadth = center.shape
    other_rows = other.shape[1]
    parts = breadth // LANES
    height = padded_rows - 2 * EDGE
    shape = jax.ShapeDtypeStruct((2, height, breadth), jnp.float32)
    vmem = pl.BlockSpec(memory_space=pltpu.VMEM)
    return pl.pallas_call(
        flow_kernel,
        out_shape=(shape, shape),
        in_specs=[vmem, vmem],
        out_specs=(vmem, vmem),
        scratch_shapes=[
            pltpu.VMEM((channels, parts, padded_rows + 8, LANES), jnp.float32),
            pltpu.VMEM((channels, parts, other_rows, LANES), jnp.float32),
            pltpu.VMEM((SPAN, SPAN, parts, padded_rows + 8, LANES), jnp.float32),
            pltpu.VMEM((parts, height, LANES), jnp.float32),
            pltpu.VMEM((parts, height, LANES), jnp.float32),
        ],
        compiler_params=pltpu.CompilerParams(vmem_limit_bytes=48 * 1024 * 1024),
    )(center, other)


def sent(value, up, along):
    axes = ("gz", "xy", "col")
    sections = lax.axis_size("gz")
    tiles = lax.axis_size(("xy", "col"))
    pairs = [
        (z * tiles + t, (z + up) * tiles + t + along)
        for z in range(sections)
        for t in range(tiles)
        if 0 <= z + up < sections and 0 <= t + along < tiles
    ]
    return lax.ppermute(value, axes, pairs)


def margins(middle, before, after, edge):
    channels, rows, breadth = middle.shape
    blank = jnp.zeros((channels, edge - RADIUS, breadth), middle.dtype)
    return jnp.concatenate([blank, before, middle, after, blank], axis=1)


def spread(first, second):
    return lax.rsqrt(1.0 + (first * first + second * second) / (saturation * saturation))


def relax_kernel(
    links_ref,
    forward_ref,
    ahead_ref,
    stiff_ref,
    out_ref,
    stiff,
    disp,
    prior,
    backward,
    summed,
    summed_in,
    above,
    below,
    rounded,
    above_in,
    below_in,
    flow_send,
    flow_recv,
    sum_send,
    sum_recv,
    stiff_send,
    stiff_recv,
    row_send,
    row_recv,
    sect_send,
    sect_recv,
):
    height, breadth = stiff_ref.shape
    sections = lax.axis_size("gz")
    wide = lax.axis_size("col")
    tiles = lax.axis_size("xy") * wide
    section = lax.axis_index("gz")
    tile = lax.axis_index("xy") * wide + lax.axis_index("col")
    link_here = links_ref[0]
    link_below = links_ref[1]

    def tile_at(t):
        return {"xy": t // wide, "col": lax.rem(t, wide)}

    next_tile, prior_tile = tile_at(tile + 1), tile_at(tile + tiles - 1 - tiles * (tile > 0))
    next_section, prior_section = {"gz": section + 1}, {"gz": section - 1}
    has_next_tile, has_prior_tile = tile + 1 < tiles, tile > 0
    has_next, has_prior = section + 1 < sections, section > 0
    partners = (
        (has_next_tile, next_tile),
        (has_prior_tile, prior_tile),
        (has_next, next_section),
        (has_prior, prior_section),
    )

    top, bottom = slice(0, EDGE), slice(EDGE + height, 2 * EDGE + height)
    first, last = slice(EDGE, 2 * EDGE), slice(height, EDGE + height)
    for edge in (top, bottom):
        stiff[edge, :] = jnp.zeros((EDGE, breadth), jnp.float32)
        for step in range(STEPS):
            for part in range(2):
                disp[step, part, edge, :] = jnp.zeros((EDGE, breadth), jnp.float32)
    for array in (prior, backward, summed_in):
        array[...] = jnp.zeros(array.shape, array.dtype)
    above_in[...] = jnp.zeros(above_in.shape, above_in.dtype)
    below_in[...] = jnp.zeros(below_in.shape, below_in.dtype)
    stiff[EDGE : EDGE + height, :] = stiff_ref[...]

    barrier = pltpu.get_barrier_semaphore()
    count = jnp.int32(0)
    for present, partner in partners:
        count = count + present.astype(jnp.int32)

        @pl.when(present)
        def _():
            pl.semaphore_signal(
                barrier, inc=1, device_id=partner, device_id_type=pl.DeviceIdType.MESH
            )

    pl.semaphore_wait(barrier, count)

    pending = []

    def send(condition, source, target, send_sem, recv_sem, partner):
        copy = pltpu.make_async_remote_copy(
            src_ref=source,
            dst_ref=target,
            send_sem=send_sem,
            recv_sem=recv_sem,
            device_id=partner,
            device_id_type=pl.DeviceIdType.MESH,
        )

        @pl.when(condition)
        def _():
            copy.start()

        pending.append((condition, copy))
        return copy

    def arrive(condition, copy):
        @pl.when(condition)
        def _():
            copy.wait_recv()

    flows = []
    for part in range(2):
        pieces = []
        for which, (source, target) in enumerate(((forward_ref, prior), (ahead_ref, backward))):
            pieces.append(
                send(
                    has_next,
                    source.at[part],
                    target.at[part],
                    flow_send.at[part, which],
                    flow_recv.at[part, which],
                    next_section,
                )
            )
        flows.append(pieces)
    stiff_down = send(
        has_next_tile, stiff.at[last], stiff.at[top], stiff_send.at[0], stiff_recv.at[0], next_tile
    )
    stiff_up = send(
        has_prior_tile, stiff.at[first], stiff.at[bottom], stiff_send.at[1], stiff_recv.at[1], prior_tile
    )

    def send_rows(step):
        down = send(
            has_next_tile,
            disp.at[step, :, last],
            disp.at[step, :, top],
            row_send.at[step, 0],
            row_recv.at[step, 0],
            next_tile,
        )
        up = send(
            has_prior_tile,
            disp.at[step, :, first],
            disp.at[step, :, bottom],
            row_send.at[step, 1],
            row_recv.at[step, 1],
            prior_tile,
        )
        return down, up

    for part in range(2):
        for copy in flows[part]:
            arrive(has_prior, copy)
        chain = pltpu.make_async_remote_copy(
            src_ref=summed.at[part],
            dst_ref=summed_in.at[part],
            send_sem=sum_send.at[part],
            recv_sem=sum_recv.at[part],
            device_id=next_section,
            device_id_type=pl.DeviceIdType.MESH,
        )
        arrive(section > 1, chain)
        before = summed_in[part]
        here = before + link_below * (prior[part] - backward[part])
        summed[part] = here
        send(
            has_next & has_prior,
            summed.at[part],
            summed_in.at[part],
            sum_send.at[part],
            sum_recv.at[part],
            next_section,
        )
        disp[0, part, EDGE : EDGE + height, :] = 0.5 * here
        below[part] = 0.5 * before
        above[part] = 0.5 * (here + link_here * (forward_ref[part] - ahead_ref[part]))

    rows = send_rows(0)
    arrive(has_prior_tile, stiff_down)
    arrive(has_next_tile, stiff_up)
    lane = lax.broadcasted_iota(jnp.int32, (16, breadth), 1)
    at_left, at_right = lane == 0, lane == breadth - 1

    def left_of(value):
        return jnp.where(at_left, 0.0, pltpu.roll(value, 1, 1))

    def right_of(value):
        return jnp.where(at_right, 0.0, pltpu.roll(value, breadth - 1, 1))

    crossing = None
    for step in range(STEPS):
        arrive(has_prior_tile, rows[0])
        arrive(has_next_tile, rows[1])
        if crossing is not None:
            arrive(has_next, crossing[0])
            arrive(has_prior, crossing[1])

        @pl.loop(0, height // 16)
        def _(block):
            base = pl.multiple_of(block * 16, 16)
            here = pl.ds(base, 16)
            inner = pl.ds(pl.multiple_of(base + EDGE, EDGE), 16)
            around = pl.ds(base, 16 + 2 * EDGE)
            stiff_all = stiff[around, :]
            middle_stiff = stiff_all[EDGE : EDGE + 16]
            weights = [
                0.5 * (middle_stiff + neighbour)
                for neighbour in (
                    stiff_all[EDGE + 1 : EDGE + 17],
                    stiff_all[EDGE - 1 : EDGE + 15],
                    right_of(middle_stiff),
                    left_of(middle_stiff),
                )
            ]
            windows = [disp[step, part, around, :] for part in range(2)]
            middles = [window[EDGE : EDGE + 16] for window in windows]
            if step == 0:
                uppers = [above[part, here, :] for part in range(2)]
                lowers = [below[part, here, :] for part in range(2)]
            else:
                uppers = [above_in[step - 1, part, here, :].astype(jnp.float32) for part in range(2)]
                lowers = [below_in[step - 1, part, here, :].astype(jnp.float32) for part in range(2)]
            gradients = []
            for part in range(2):
                middle = middles[part]
                neighbours = (
                    windows[part][EDGE + 1 : EDGE + 17],
                    windows[part][EDGE - 1 : EDGE + 15],
                    right_of(middle),
                    left_of(middle),
                )
                total = weights[0] * (middle - neighbours[0])
                for k in range(1, 4):
                    total = total + weights[k] * (middle - neighbours[k])
                gradients.append(total)
            for sign, link, others, flow in (
                (-1.0, link_here, uppers, forward_ref),
                (-1.0, link_below, lowers, backward),
                (1.0, link_below, lowers, prior),
                (1.0, link_here, uppers, ahead_ref),
            ):
                vector = [
                    -sign * (others[part] - middles[part]) - flow[part, here, :] for part in range(2)
                ]
                scale = (sign * link) * spread(*vector)
                for part in range(2):
                    gradients[part] = gradients[part] + scale * vector[part]
            for part in range(2):
                updated = middles[part] - step_size * gradients[part]
                if step == STEPS - 1:
                    out_ref[part, here, :] = updated
                else:
                    disp[step + 1, part, inner, :] = updated
                    rounded[step, part, here, :] = updated.astype(rounded.dtype)

        if step < STEPS - 1:
            crossing = (
                send(
                    has_prior,
                    rounded.at[step],
                    above_in.at[step],
                    sect_send.at[step, 0],
                    sect_recv.at[step, 0],
                    prior_section,
                ),
                send(
                    has_next,
                    rounded.at[step],
                    below_in.at[step],
                    sect_send.at[step, 1],
                    sect_recv.at[step, 1],
                    next_section,
                ),
            )
            rows = send_rows(step + 1)

    for condition, copy in pending:

        @pl.when(condition)
        def _():
            copy.wait_send()


def relaxed(links, forward, ahead, stiff_field):
    height, breadth = stiff_field.shape
    vmem = pl.BlockSpec(memory_space=pltpu.VMEM)
    pair = (2, height, breadth)
    moved = (STEPS - 1, 2, height, breadth)
    dma = pltpu.SemaphoreType.DMA
    return pl.pallas_call(
        relax_kernel,
        out_shape=jax.ShapeDtypeStruct(pair, jnp.float32),
        in_specs=[pl.BlockSpec(memory_space=pltpu.SMEM), vmem, vmem, vmem],
        out_specs=vmem,
        scratch_shapes=[
            pltpu.VMEM((height + 2 * EDGE, breadth), jnp.float32),
            pltpu.VMEM((STEPS, 2, height + 2 * EDGE, breadth), jnp.float32),
            *[pltpu.VMEM(pair, jnp.float32) for _ in range(6)],
            *[pltpu.VMEM(moved, jnp.bfloat16) for _ in range(3)],
            dma((2, 2)),
            dma((2, 2)),
            dma((2,)),
            dma((2,)),
            dma((2,)),
            dma((2,)),
            dma((STEPS, 2)),
            dma((STEPS, 2)),
            dma((STEPS - 1, 2)),
            dma((STEPS - 1, 2)),
        ],
        compiler_params=pltpu.CompilerParams(
            collective_id=0, has_side_effects=True, vmem_limit_bytes=16 * 1024 * 1024
        ),
    )(links, forward, ahead, stiff_field)


def on_device(features, class_map, stiffness, valid):
    center = features[0]
    height, breadth = (center.shape[1], center.shape[2])
    section = lax.axis_index("gz")
    tile_index = lax.axis_index(("xy", "col"))
    column = lax.dynamic_slice_in_dim(valid, tile_index, 1, 1)[:, 0].astype(jnp.float32)
    link_all = column * jnp.concatenate([column[1:], jnp.zeros((1,), jnp.float32)])
    link_here = lax.dynamic_index_in_dim(link_all, section, 0, keepdims=False)
    link_below = jnp.where(
        section > 0,
        lax.dynamic_index_in_dim(link_all, jnp.maximum(section - 1, 0), 0, keepdims=False),
        0.0,
    )
    head, tail = (center[:, :RADIUS], center[:, height - RADIUS :])
    other = margins(sent(center, -1, 0), sent(tail, -1, 1), sent(head, -1, -1), 2 * EDGE)
    padded = margins(center, sent(tail, 0, 1), sent(head, 0, -1), EDGE)
    forward, ahead_flow = flows_between(padded, other)
    levels = jnp.arange(stiffness.shape[0], dtype=jnp.int32)
    stiff_field = jnp.sum(
        jnp.where(class_map[0][None] == levels[:, None, None], stiffness[:, None, None], 0.0),
        axis=0,
    )
    displace = relaxed(jnp.stack([link_here, link_below]), forward, ahead_flow, stiff_field)
    return (displace[None], forward[None])


def solution(mesh):
    placed = (
        P(("groups", "gz"), None, ("xy", "col"), None),
        P(("groups", "gz"), ("xy", "col"), None),
        P(),
        P("groups", None),
    )
    return jax.shard_map(
        on_device,
        mesh=mesh,
        in_specs=placed,
        out_specs=(
            P(("groups", "gz"), None, ("xy", "col"), None),
            P(("groups", "gz"), None, ("xy", "col"), None),
        ),
        check_vma=False,
    )
```

```python
import math

import jax
import jax.numpy as jnp
from jax import lax
from jax.experimental import pallas as pl
from jax.experimental.pallas import tpu as pltpu
from jax.sharding import PartitionSpec as P

RADIUS = 6
STEPS = 3


score_scale = 0.25
step_size = 0.1
saturation = 2.0


LANES = 128
EDGE = 8
SPAN = 2 * RADIUS + 1
GROUP = 4
MANY = 8


def shifted(halves, turn, from_lower, from_upper):
    count = len(halves)
    turned = [pltpu.roll(half, turn, 1) for half in halves]
    blank = jnp.zeros_like(turned[0])
    results = []
    for k in range(count):
        lower = turned[k - 1] if k > 0 else blank
        upper = turned[k + 1] if k + 1 < count else blank
        results.append(jnp.where(from_lower, lower, jnp.where(from_upper, upper, turned[k])))
    return results


def flow_kernel(
    center_ref, other_ref, forward_ref, ahead_ref, center, turned, score_f, top_f, top_b
):
    channels, padded_rows, breadth = center_ref.shape
    parts = breadth // LANES
    height = padded_rows - 2 * EDGE
    other_rows = other_ref.shape[1]
    lane = lax.broadcasted_iota(jnp.int32, (8, LANES), 1)
    many = math.gcd(height // 8, MANY)
    together = math.gcd(channels, 16)
    factor = score_scale * math.log2(math.e)

    @pl.loop(0, channels)
    def _(c):
        for k in range(parts):
            cols = slice(k * LANES, (k + 1) * LANES)
            center[c, k, 0:padded_rows, :] = center_ref[c, :, cols].astype(jnp.float32) * factor

    top_f[...] = jnp.full(top_f.shape, -jnp.inf, jnp.float32)
    top_b[...] = jnp.full(top_b.shape, -jnp.inf, jnp.float32)

    @pl.loop(0, SPAN)
    def _(col):
        shift = col - RADIUS
        back_turn = lax.rem(LANES + shift, LANES)
        back_masks = (lane - shift < 0, lane - shift >= LANES)
        source = lax.broadcasted_iota(jnp.int32, (breadth, breadth), 0)
        target = lax.broadcasted_iota(jnp.int32, (breadth, breadth), 1)
        mover = jnp.where(source - target == shift, 1.0, 0.0).astype(jnp.bfloat16)

        @pl.loop(0, channels // together)
        def _(group):
            these = pl.ds(group * together, together)
            moved = jnp.dot(
                other_ref[these].reshape(together * other_rows, breadth),
                mover,
                preferred_element_type=jnp.float32,
            ).reshape(together, other_rows, breadth)
            for k in range(parts):
                turned[these, k] = moved[:, :, k * LANES : (k + 1) * LANES]

        @pl.loop(0, padded_rows // 16)
        def _(pair):
            base = pl.multiple_of(pair * 16, 16)
            for k in range(parts):
                sums = [[None] * SPAN for _ in range(2)]
                for c in range(channels):
                    mine = {}
                    windows = {}
                    for j in range(2):
                        for row in range(SPAN):
                            near = (RADIUS - (row - RADIUS)) % GROUP
                            far = 8 * j + EDGE + row - RADIUS + near
                            if (j, near) not in mine:
                                mine[j, near] = center[c, k, pl.ds(base + 8 * j + near, 8), :]
                            if far not in windows:
                                windows[far] = turned[c, k, pl.ds(base + far, 8), :]
                            term = mine[j, near] * windows[far]
                            sums[j][row] = term if c == 0 else sums[j][row] + term
                for j in range(2):
                    for row in range(SPAN):
                        near = (RADIUS - (row - RADIUS)) % GROUP
                        score_f[col, row, k, pl.ds(base + 8 * j + near, 8), :] = sums[j][row]

        @pl.loop(0, height // (8 * many))
        def _(chunk):
            raw = []
            for j in range(many):
                base = pl.multiple_of(chunk * (8 * many) + 8 * j, 8)
                here = pl.ds(base, 8)
                bests_f, bests_b = [None] * parts, [None] * parts
                for k in range(parts):
                    for row in range(SPAN):
                        value = score_f[col, row, k, pl.ds(base + EDGE, 8), :]
                        other = score_f[col, row, k, pl.ds(base + EDGE + RADIUS - row, 8), :]
                        bests_f[k] = value if row == 0 else jnp.maximum(bests_f[k], value)
                        bests_b[k] = other if row == 0 else jnp.maximum(bests_b[k], other)
                    top_f[k, here, :] = jnp.maximum(top_f[k, here, :], bests_f[k])
                raw.append((here, bests_b))
            turned_back = [(here, shifted(values, back_turn, *back_masks)) for here, values in raw]
            for here, values in turned_back:
                for k in range(parts):
                    top_b[k, here, :] = jnp.maximum(top_b[k, here, :], values[k])

    @pl.loop(0, height // (8 * many))
    def _(chunk):
        bases = [pl.multiple_of(chunk * (8 * many) + 8 * j, 8) for j in range(many)]
        bests_f = [[top_f[k, pl.ds(base, 8), :] for k in range(parts)] for base in bases]
        bests_b = [[top_b[k, pl.ds(base, 8), :] for k in range(parts)] for base in bases]

        def sums_of(scores, best, sign):
            weights = [jnp.exp2(score - best) for score in scores]
            summed = weights[RADIUS]
            lean = None
            for step in range(1, RADIUS + 1):
                up, down = weights[RADIUS + step], weights[RADIUS - step]
                summed = summed + (up + down)
                part = (up - down) * (sign * step)
                lean = part if lean is None else lean + part
            return summed, lean

        def one_column(col, carry):
            shift = col - RADIUS
            place = shift.astype(jnp.float32)
            forth_turn = lax.rem(LANES - shift, LANES)
            back_turn = lax.rem(LANES + shift, LANES)
            forth_masks = (lane + shift < 0, lane + shift >= LANES)
            back_masks = (lane - shift < 0, lane - shift >= LANES)
            moved = [shifted(best, forth_turn, *forth_masks) for best in bests_b]
            forward = [
                [
                    sums_of(
                        [score_f[col, row, k, pl.ds(base + EDGE, 8), :] for row in range(SPAN)],
                        bests_f[j][k],
                        1.0,
                    )
                    for k in range(parts)
                ]
                for j, base in enumerate(bases)
            ]
            back = [
                [
                    sums_of(
                        [
                            score_f[col, row, k, pl.ds(base + EDGE + RADIUS - row, 8), :]
                            for row in range(SPAN)
                        ],
                        moved[j][k],
                        -1.0,
                    )
                    for k in range(parts)
                ]
                for j, base in enumerate(bases)
            ]
            turned_back = [
                [shifted([value[i] for value in row], back_turn, *back_masks) for i in range(2)]
                for row in back
            ]
            results = []
            for j in range(many):
                for k in range(parts):
                    column = lane + (k * LANES - shift)
                    inside = (column >= 0) & (column < breadth)
                    outside = float(SPAN) * jnp.exp2(-bests_b[j][k])
                    summed = jnp.where(inside, turned_back[j][0][k], outside)
                    lean = jnp.where(inside, turned_back[j][1][k], 0.0)
                    old = carry[j * parts + k]
                    ahead_sum, ahead_lean = forward[j][k]
                    results.append(
                        (
                            old[0] + ahead_sum,
                            old[1] + ahead_lean,
                            old[2] + ahead_sum * place,
                            old[3] + summed,
                            old[4] + lean,
                            old[5] - summed * place,
                        )
                    )
            return tuple(results)

        zero = jnp.zeros((8, LANES), jnp.float32)
        results = lax.fori_loop(0, SPAN, one_column, ((zero,) * 6,) * (many * parts))
        for j, base in enumerate(bases):
            for k in range(parts):
                cols = slice(k * LANES, (k + 1) * LANES)
                sums = results[j * parts + k]
                for out_ref, (total, along_rows, along_cols) in (
                    (forward_ref, sums[:3]),
                    (ahead_ref, sums[3:]),
                ):
                    out_ref[0, pl.ds(base, 8), cols] = along_rows / total
                    out_ref[1, pl.ds(base, 8), cols] = along_cols / total


def flows_between(center, other):
    channels, padded_rows, breadth = center.shape
    other_rows = other.shape[1]
    parts = breadth // LANES
    height = padded_rows - 2 * EDGE
    shape = jax.ShapeDtypeStruct((2, height, breadth), jnp.float32)
    vmem = pl.BlockSpec(memory_space=pltpu.VMEM)
    return pl.pallas_call(
        flow_kernel,
        out_shape=(shape, shape),
        in_specs=[vmem, vmem],
        out_specs=(vmem, vmem),
        scratch_shapes=[
            pltpu.VMEM((channels, parts, padded_rows + 8, LANES), jnp.float32),
            pltpu.VMEM((channels, parts, other_rows, LANES), jnp.float32),
            pltpu.VMEM((SPAN, SPAN, parts, padded_rows + 8, LANES), jnp.float32),
            pltpu.VMEM((parts, height, LANES), jnp.float32),
            pltpu.VMEM((parts, height, LANES), jnp.float32),
        ],
        compiler_params=pltpu.CompilerParams(vmem_limit_bytes=48 * 1024 * 1024),
    )(center, other)


def sent(value, up, along):
    axes = ("gz", "xy", "col")
    sections = lax.axis_size("gz")
    tiles = lax.axis_size(("xy", "col"))
    pairs = [
        (z * tiles + t, (z + up) * tiles + t + along)
        for z in range(sections)
        for t in range(tiles)
        if 0 <= z + up < sections and 0 <= t + along < tiles
    ]
    return lax.ppermute(value, axes, pairs)


def margins(middle, before, after, edge):
    channels, rows, breadth = middle.shape
    blank = jnp.zeros((channels, edge - RADIUS, breadth), middle.dtype)
    return jnp.concatenate([blank, before, middle, after, blank], axis=1)


def spread(first, second):
    return lax.rsqrt(1.0 + (first * first + second * second) / (saturation * saturation))


def relax_kernel(
    links_ref,
    forward_ref,
    ahead_ref,
    stiff_ref,
    out_ref,
    stiff,
    disp,
    prior,
    backward,
    summed,
    summed_in,
    above,
    below,
    excess,
    rounded,
    above_in,
    below_in,
    flow_send,
    flow_recv,
    sum_send,
    sum_recv,
    stiff_send,
    stiff_recv,
    row_send,
    row_recv,
    sect_send,
    sect_recv,
):
    height, breadth = stiff_ref.shape
    sections = lax.axis_size("gz")
    wide = lax.axis_size("col")
    tiles = lax.axis_size("xy") * wide
    section = lax.axis_index("gz")
    tile = lax.axis_index("xy") * wide + lax.axis_index("col")
    link_here = links_ref[0]
    link_below = links_ref[1]

    def tile_at(t):
        return {"xy": t // wide, "col": lax.rem(t, wide)}

    next_tile, prior_tile = tile_at(tile + 1), tile_at(tile + tiles - 1 - tiles * (tile > 0))
    next_section, prior_section = {"gz": section + 1}, {"gz": section - 1}
    has_next_tile, has_prior_tile = tile + 1 < tiles, tile > 0
    has_next, has_prior = section + 1 < sections, section > 0
    partners = (
        (has_next_tile, next_tile),
        (has_prior_tile, prior_tile),
        (has_next, next_section),
        (has_prior, prior_section),
    )

    top, bottom = slice(0, EDGE), slice(EDGE + height, 2 * EDGE + height)
    first, last = slice(EDGE, 2 * EDGE), slice(height, EDGE + height)
    for edge in (top, bottom):
        stiff[edge, :] = jnp.zeros((EDGE, breadth), jnp.float32)
        for step in range(STEPS):
            for part in range(2):
                disp[step, part, edge, :] = jnp.zeros((EDGE, breadth), jnp.float32)
    for absent, arrays in (
        (section == 0, (prior, backward, below_in)),
        (section < 2, (summed_in,)),
        (section == sections - 1, (above_in,)),
    ):

        @pl.when(absent)
        def _():
            for array in arrays:
                array[...] = jnp.zeros(array.shape, array.dtype)

    excess[...] = link_here * (forward_ref[...] - ahead_ref[...])
    stiff[EDGE : EDGE + height, :] = stiff_ref[...]

    barrier = pltpu.get_barrier_semaphore()
    count = jnp.int32(0)
    for present, partner in partners:
        count = count + present.astype(jnp.int32)

        @pl.when(present)
        def _():
            pl.semaphore_signal(
                barrier, inc=1, device_id=partner, device_id_type=pl.DeviceIdType.MESH
            )

    pl.semaphore_wait(barrier, count)

    pending = []

    def send(condition, source, target, send_sem, recv_sem, partner):
        copy = pltpu.make_async_remote_copy(
            src_ref=source,
            dst_ref=target,
            send_sem=send_sem,
            recv_sem=recv_sem,
            device_id=partner,
            device_id_type=pl.DeviceIdType.MESH,
        )

        @pl.when(condition)
        def _():
            copy.start()

        pending.append((condition, copy))
        return copy

    def arrive(condition, copy):
        @pl.when(condition)
        def _():
            copy.wait_recv()

    terms, flows = [
        [
            send(
                has_next,
                source.at[part],
                target.at[part],
                flow_send.at[part, which],
                flow_recv.at[part, which],
                next_section,
            )
            for part in range(2)
        ]
        for which, (source, target) in enumerate(((excess, backward), (forward_ref, prior)))
    ]
    stiff_down = send(
        has_next_tile, stiff.at[last], stiff.at[top], stiff_send.at[0], stiff_recv.at[0], next_tile
    )
    stiff_up = send(
        has_prior_tile, stiff.at[first], stiff.at[bottom], stiff_send.at[1], stiff_recv.at[1], prior_tile
    )

    def send_rows(step):
        down = send(
            has_next_tile,
            disp.at[step, :, last],
            disp.at[step, :, top],
            row_send.at[step, 0],
            row_recv.at[step, 0],
            next_tile,
        )
        up = send(
            has_prior_tile,
            disp.at[step, :, first],
            disp.at[step, :, bottom],
            row_send.at[step, 1],
            row_recv.at[step, 1],
            prior_tile,
        )
        return down, up

    for part in range(2):
        arrive(has_prior, terms[part])
        chain = pltpu.make_async_remote_copy(
            src_ref=summed.at[part],
            dst_ref=summed_in.at[part],
            send_sem=sum_send.at[part],
            recv_sem=sum_recv.at[part],
            device_id=next_section,
            device_id_type=pl.DeviceIdType.MESH,
        )
        arrive(section > 1, chain)
        before = summed_in[part]
        here = before + backward[part]
        summed[part] = here
        send(
            has_next & has_prior,
            summed.at[part],
            summed_in.at[part],
            sum_send.at[part],
            sum_recv.at[part],
            next_section,
        )
        disp[0, part, EDGE : EDGE + height, :] = 0.5 * here
        below[part] = 0.5 * before
        above[part] = 0.5 * (here + excess[part])

    rows = send_rows(0)
    for part in range(2):
        arrive(has_prior, flows[part])
        backward[part] = prior[part] - backward[part]
    arrive(has_prior_tile, stiff_down)
    arrive(has_next_tile, stiff_up)
    lane = lax.broadcasted_iota(jnp.int32, (16, breadth), 1)
    at_left, at_right = lane == 0, lane == breadth - 1

    def left_of(value):
        return jnp.where(at_left, 0.0, pltpu.roll(value, 1, 1))

    def right_of(value):
        return jnp.where(at_right, 0.0, pltpu.roll(value, breadth - 1, 1))

    crossing = None
    for step in range(STEPS):
        arrive(has_prior_tile, rows[0])
        arrive(has_next_tile, rows[1])
        if crossing is not None:
            arrive(has_next, crossing[0])
            arrive(has_prior, crossing[1])

        @pl.loop(0, height // 16)
        def _(block):
            base = pl.multiple_of(block * 16, 16)
            here = pl.ds(base, 16)
            inner = pl.ds(pl.multiple_of(base + EDGE, EDGE), 16)
            around = pl.ds(base, 16 + 2 * EDGE)
            stiff_all = stiff[around, :]
            middle_stiff = stiff_all[EDGE : EDGE + 16]
            weights = [
                0.5 * (middle_stiff + neighbour)
                for neighbour in (
                    stiff_all[EDGE + 1 : EDGE + 17],
                    stiff_all[EDGE - 1 : EDGE + 15],
                    right_of(middle_stiff),
                    left_of(middle_stiff),
                )
            ]
            windows = [disp[step, part, around, :] for part in range(2)]
            middles = [window[EDGE : EDGE + 16] for window in windows]
            if step == 0:
                uppers = [above[part, here, :] for part in range(2)]
                lowers = [below[part, here, :] for part in range(2)]
            else:
                uppers = [above_in[step - 1, part, here, :].astype(jnp.float32) for part in range(2)]
                lowers = [below_in[step - 1, part, here, :].astype(jnp.float32) for part in range(2)]
            gradients = []
            for part in range(2):
                middle = middles[part]
                neighbours = (
                    windows[part][EDGE + 1 : EDGE + 17],
                    windows[part][EDGE - 1 : EDGE + 15],
                    right_of(middle),
                    left_of(middle),
                )
                total = weights[0] * (middle - neighbours[0])
                for k in range(1, 4):
                    total = total + weights[k] * (middle - neighbours[k])
                gradients.append(total)
            for sign, link, others, flow in (
                (-1.0, link_here, uppers, forward_ref),
                (-1.0, link_below, lowers, backward),
                (1.0, link_below, lowers, prior),
                (1.0, link_here, uppers, ahead_ref),
            ):
                vector = [
                    -sign * (others[part] - middles[part]) - flow[part, here, :] for part in range(2)
                ]
                scale = (sign * link) * spread(*vector)
                for part in range(2):
                    gradients[part] = gradients[part] + scale * vector[part]
            for part in range(2):
                updated = middles[part] - step_size * gradients[part]
                if step == STEPS - 1:
                    out_ref[part, here, :] = updated
                else:
                    disp[step + 1, part, inner, :] = updated
                    rounded[step, part, here, :] = updated.astype(rounded.dtype)

        if step < STEPS - 1:
            crossing = (
                send(
                    has_prior,
                    rounded.at[step],
                    above_in.at[step],
                    sect_send.at[step, 0],
                    sect_recv.at[step, 0],
                    prior_section,
                ),
                send(
                    has_next,
                    rounded.at[step],
                    below_in.at[step],
                    sect_send.at[step, 1],
                    sect_recv.at[step, 1],
                    next_section,
                ),
            )
            rows = send_rows(step + 1)

    for condition, copy in pending:

        @pl.when(condition)
        def _():
            copy.wait_send()


def relaxed(links, forward, ahead, stiff_field):
    height, breadth = stiff_field.shape
    vmem = pl.BlockSpec(memory_space=pltpu.VMEM)
    pair = (2, height, breadth)
    moved = (STEPS - 1, 2, height, breadth)
    dma = pltpu.SemaphoreType.DMA
    return pl.pallas_call(
        relax_kernel,
        out_shape=jax.ShapeDtypeStruct(pair, jnp.float32),
        in_specs=[pl.BlockSpec(memory_space=pltpu.SMEM), vmem, vmem, vmem],
        out_specs=vmem,
        scratch_shapes=[
            pltpu.VMEM((height + 2 * EDGE, breadth), jnp.float32),
            pltpu.VMEM((STEPS, 2, height + 2 * EDGE, breadth), jnp.float32),
            *[pltpu.VMEM(pair, jnp.float32) for _ in range(7)],
            *[pltpu.VMEM(moved, jnp.bfloat16) for _ in range(3)],
            dma((2, 2)),
            dma((2, 2)),
            dma((2,)),
            dma((2,)),
            dma((2,)),
            dma((2,)),
            dma((STEPS, 2)),
            dma((STEPS, 2)),
            dma((STEPS - 1, 2)),
            dma((STEPS - 1, 2)),
        ],
        compiler_params=pltpu.CompilerParams(
            collective_id=0, has_side_effects=True, vmem_limit_bytes=16 * 1024 * 1024
        ),
    )(links, forward, ahead, stiff_field)


def on_device(features, class_map, stiffness, valid):
    center = features[0]
    height, breadth = (center.shape[1], center.shape[2])
    section = lax.axis_index("gz")
    tile_index = lax.axis_index(("xy", "col"))
    column = lax.dynamic_slice_in_dim(valid, tile_index, 1, 1)[:, 0].astype(jnp.float32)
    link_all = column * jnp.concatenate([column[1:], jnp.zeros((1,), jnp.float32)])
    link_here = lax.dynamic_index_in_dim(link_all, section, 0, keepdims=False)
    link_below = jnp.where(
        section > 0,
        lax.dynamic_index_in_dim(link_all, jnp.maximum(section - 1, 0), 0, keepdims=False),
        0.0,
    )
    head, tail = (center[:, :RADIUS], center[:, height - RADIUS :])
    other = margins(sent(center, -1, 0), sent(tail, -1, 1), sent(head, -1, -1), 2 * EDGE)
    padded = margins(center, sent(tail, 0, 1), sent(head, 0, -1), EDGE)
    forward, ahead_flow = flows_between(padded, other)
    levels = jnp.arange(stiffness.shape[0], dtype=jnp.int32)
    stiff_field = jnp.sum(
        jnp.where(class_map[0][None] == levels[:, None, None], stiffness[:, None, None], 0.0),
        axis=0,
    )
    displace = relaxed(jnp.stack([link_here, link_below]), forward, ahead_flow, stiff_field)
    return (displace[None], forward[None])


def solution(mesh):
    placed = (
        P(("groups", "gz"), None, ("xy", "col"), None),
        P(("groups", "gz"), ("xy", "col"), None),
        P(),
        P("groups", None),
    )
    return jax.shard_map(
        on_device,
        mesh=mesh,
        in_specs=placed,
        out_specs=(
            P(("groups", "gz"), None, ("xy", "col"), None),
            P(("groups", "gz"), None, ("xy", "col"), None),
        ),
        check_vma=False,
    )
```
